1024 devices in a mesh: blk: 128 (over y_hi, z, x), rep: 8 (over y_lo, core).
Axes of the slice: x: 4, y: 8 (y_hi: 2, y_lo: 4; y = y_hi * 4 + y_lo), z: 16, core: 2. Of those that a mesh axis runs over, the one named last changes fastest.
Arguments:
- features: bfloat16 [32768, 256], P(('blk', 'rep')), may hold values from -6 to 6
- weight: bfloat16 [256, 256], replicated, may hold values from -0.375 to 0.375
- cotangent: bfloat16 [32768, 256], P('blk'), may hold values from -6 to 6
- tile_values: bfloat16 [128, 8, 2, 96, 32, 128], P('blk', 'rep'), may hold values from 0 to 0.3
- tile_counts: int32 [128, 8, 2, 96], P('blk', 'rep'), may hold values from 0 to 32, as said below
- tile_blocks: int32 [128, 8, 2, 96], P('blk', 'rep'), may hold values from 0 to 127, as said below
Outputs:
- activations: bfloat16 [32768, 256], P(('blk', 'rep'))
- grad_features: bfloat16 [32768, 256], P(('blk', 'rep'))
- grad_weight: float32 [256, 256], replicated
The draws below stay inside these ranges and needn't reach their ends.
Inputs may be any that keep to these rules, and one draw needn't show every extreme that they name: `tile_counts`: in each row tile of a panel and replica group, the slots below some number hold counts of 1 to 32 and the others 0; slot 0 holds 32, and in some row tile all 96 slots hold nonzero counts. `tile_blocks`: in each row tile of a panel and replica group the 96 slots name distinct source blocks.
All inputs are finite; a program needn't handle non-finite values.
Results may differ from the reference program's by a relative error of at most 0.0062.
Values may be sent and summed in bfloat16 or wider, within the bound.
No kernel may reach another device: no remote copies, remote signals or barrier semaphores. Data moves between devices by JAX's collectives and lax.ppermute only.
A program may use at most 32 MiB of HBM per device.

```python
import jax
import jax.numpy as jnp
from jax import lax

F = 256
TILE = 128
ROWS_DEV = 32
PANELS = 128
REPLICAS = 8
ROW_TILES = 2
NODES = 32768
MAXLIVE = 96


def draw_tile_values(key, part):
    key = jax.random.fold_in(key, 3)
    key_edge, key_size = jax.random.split(key, 2)
    shape = (PANELS, REPLICAS, ROW_TILES, MAXLIVE, ROWS_DEV, TILE)
    divisor = max(1, REPLICAS * MAXLIVE * ROWS_DEV // 160)
    edges = jax.random.randint(key_edge, shape, 0, divisor) == 0
    magnitude = jax.random.uniform(key_size, shape, jnp.float32, 0.08, 0.24)
    return jnp.where(edges, magnitude, 0.0).astype(jnp.bfloat16)


def draw_tile_counts(key, part):
    key = jax.random.fold_in(key, 7)
    key_div, key_pick, key_fill = jax.random.split(key, 3)
    groups = PANELS * REPLICAS
    rows_all = groups * ROW_TILES
    divisor = jax.random.randint(key_div, (groups, 1), 1, 5)
    totals = jnp.broadcast_to(MAXLIVE // divisor, (groups, ROW_TILES)).reshape(rows_all)
    chosen = jax.random.randint(key_pick, (), 0, rows_all)
    totals = jnp.where(jnp.arange(rows_all) == chosen, MAXLIVE, totals)
    slot_ids = jnp.arange(MAXLIVE, dtype=jnp.int32)[None, :]
    filled = jax.random.randint(key_fill, (rows_all, MAXLIVE), 1, ROWS_DEV + 1)
    filled = jnp.where(slot_ids == 0, ROWS_DEV, filled)
    counts = jnp.where(slot_ids < totals[:, None], filled, 0)
    return counts.reshape(PANELS, REPLICAS, ROW_TILES, MAXLIVE).astype(jnp.int32)


def draw_tile_blocks(key, part):
    key = jax.random.fold_in(key, 11)
    rows_all = PANELS * REPLICAS * ROW_TILES
    perm_keys = jax.random.split(key, rows_all)
    orders = jax.vmap(lambda single: jax.random.permutation(single, PANELS))(perm_keys)
    return orders[:, :MAXLIVE].reshape(PANELS, REPLICAS, ROW_TILES, MAXLIVE).astype(jnp.int32)


def block_levels(rng, shape, pieces, smallest, high):
    def one(position, shards_of):
        steps = jax.random.uniform(jax.random.fold_in(jax.random.fold_in(rng, 6), position), (shards_of,), jnp.float32, smallest / len(pieces), high / len(pieces))
        return jnp.repeat(jnp.exp(steps), shape[position] // shards_of).reshape((-1,) + (1,) * (len(shape) - position - 1))

    factor_of = one(*pieces[0])
    for cut in pieces[1:]:
        factor_of = factor_of * one(*cut)
    return factor_of


def centred(key, dims, width, bound, pieces=(), held_as=jnp.bfloat16):
    array = width * jax.random.normal(key, dims, jnp.float32)
    if pieces:
        array = array * block_levels(key, dims, pieces, -0.22, 0.18)
    return jnp.clip(array, -bound, bound).astype(held_as)


def setup_inputs(seed: int = 0) -> dict:
    keys = jax.random.split(jax.random.key(seed), 7)
    features = centred(keys[0], (NODES, F), 1.0, 6.0, ((0, 1024),))
    weight = centred(keys[1], (F, F), F ** -0.5, 0.375)
    cotangent = centred(keys[2], (NODES, F), 1.0, 6.0, ((0, 128),))
    tile_values = draw_tile_values(jax.random.fold_in(keys[6], 71), 0)
    tile_counts = draw_tile_counts(jax.random.fold_in(keys[6], 71), 0)
    tile_blocks = draw_tile_blocks(jax.random.fold_in(keys[6], 71), 0)
    return {"features": features, "weight": weight, "cotangent": cotangent, "tile_values": tile_values, "tile_counts": tile_counts, "tile_blocks": tile_blocks}


def panel_tiles(tile_values, tile_counts, tile_blocks, panel):
    values = lax.dynamic_index_in_dim(tile_values, panel, 0, keepdims=False).astype(jnp.float32)
    limit = lax.dynamic_index_in_dim(tile_counts, panel, 0, keepdims=False)
    blocks = lax.dynamic_index_in_dim(tile_blocks, panel, 0, keepdims=False)
    columns = jnp.arange(ROWS_DEV, dtype=jnp.int32)
    keep_mask = (columns < limit[..., None]).astype(jnp.float32)
    return values * keep_mask[..., None], blocks


def reference(features, weight, cotangent, tile_values, tile_counts, tile_blocks):
    sources = jnp.transpose(features.reshape(PANELS, REPLICAS, ROWS_DEV, F), (1, 0, 2, 3)).astype(jnp.float32)
    panel_ids = jnp.arange(PANELS, dtype=jnp.int32)
    rep_ids = jnp.arange(REPLICAS, dtype=jnp.int32)[:, None, None]

    def forward_panel(panel):
        tiles, blocks = panel_tiles(tile_values, tile_counts, tile_blocks, panel)
        picked = sources[rep_ids, blocks]
        return jnp.einsum("rnmct,rnmcf->ntf", tiles, picked, precision=lax.Precision.HIGHEST)

    aggregate = lax.map(forward_panel, panel_ids).reshape(NODES, F)
    aggregate_bf = aggregate.astype(jnp.bfloat16)
    preact = jnp.dot(aggregate_bf, weight, preferred_element_type=jnp.float32)
    activations = jax.nn.silu(preact).astype(jnp.bfloat16)
    sigmoid_value = jax.nn.sigmoid(preact)
    slope = (cotangent.astype(jnp.float32) * sigmoid_value * (1.0 + preact * (1.0 - sigmoid_value))).astype(jnp.bfloat16)
    grad_weight = jnp.dot(aggregate_bf.T, slope, preferred_element_type=jnp.float32) * (NODES ** -0.5)
    back_grad = jnp.dot(slope, weight.T, preferred_element_type=jnp.float32).astype(jnp.bfloat16)
    back_panels = back_grad.reshape(PANELS, ROW_TILES, TILE, F)

    def backward_step(carry, panel):
        tiles, blocks = panel_tiles(tile_values, tile_counts, tile_blocks, panel)
        grads = lax.dynamic_index_in_dim(back_panels, panel, 0, keepdims=False).astype(jnp.float32)
        contrib = jnp.einsum("rnmct,ntf->rnmcf", tiles, grads, precision=lax.Precision.HIGHEST)
        return carry.at[rep_ids, blocks].add(contrib), None

    start_carry = jnp.zeros((REPLICAS, PANELS, ROWS_DEV, F), jnp.float32)
    summed, _ = lax.scan(backward_step, start_carry, panel_ids)
    grad_features = jnp.transpose(summed, (1, 0, 2, 3)).reshape(NODES, F).astype(jnp.bfloat16)
    return activations, grad_features, grad_weight
```

```python
import functools

import jax
import jax.numpy as jnp
from jax import lax
from jax.experimental import pallas as pl
from jax.experimental.pallas import tpu as pltpu
from jax.sharding import Mesh, PartitionSpec as P

SPLIT = {"yh": 2, "z": 16, "x": 4, "yl": 4, "c": 2}
BLK = ("yh", "z", "x")
REP = ("yl", "c")
bf16 = jnp.bfloat16
f32 = jnp.float32


def exchange(chunks, axes):
    return lax.all_to_all(chunks, axes, 0, 0, tiled=True)


def gather(block, axes):
    members = lax.axis_size(axes)
    return exchange(jnp.broadcast_to(block, (members,) + block.shape), axes)


def panel_kernel(places_ref, counts_ref, tiles_ref, panel_ref):
    row_tiles, slot_count, rows, tile_size = tiles_ref.shape
    total = panel_ref.shape[0]
    step = min(total, 256)

    def clear(i, carry):
        start = pl.multiple_of(i * step, step)
        panel_ref[pl.ds(start, step), :] = jnp.zeros((step, panel_ref.shape[1]), bf16)
        return carry

    lax.fori_loop(0, total // step, clear, 0)
    columns = lax.broadcasted_iota(jnp.int32, (rows, tile_size), 0)

    def place(slot, carry):
        for n in range(row_tiles):
            start = pl.multiple_of(places_ref[n, slot] * rows, rows)
            tile = tiles_ref[n, slot].astype(f32)
            kept = jnp.where(columns < counts_ref[n, slot], tile, 0.0).astype(bf16)
            panel_ref[pl.ds(start, rows), n * tile_size : (n + 1) * tile_size] = kept
        return carry

    lax.fori_loop(0, slot_count, place, 0, unroll=8)


def dense_panel(places, counts, tiles, blocks_total):
    row_tiles, _, rows, tile_size = tiles.shape
    return pl.pallas_call(
        panel_kernel,
        out_shape=jax.ShapeDtypeStruct((blocks_total * rows, row_tiles * tile_size), bf16),
        in_specs=[
            pl.BlockSpec(memory_space=pltpu.SMEM),
            pl.BlockSpec(memory_space=pltpu.SMEM),
            pl.BlockSpec(memory_space=pltpu.VMEM),
        ],
        out_specs=pl.BlockSpec(memory_space=pltpu.VMEM),
        compiler_params=pltpu.CompilerParams(vmem_limit_bytes=16 * 1024 * 1024),
        cost_estimate=pl.CostEstimate(flops=0, bytes_accessed=4 * 1024 * 1024, transcendentals=0),
    )(places, counts, tiles)


def body(features, weight, cotangent, tile_values, tile_counts, tile_blocks):
    rows_dev, width = features.shape
    yh_n, z_n, x_n = (lax.axis_size(a) for a in BLK)
    rep_n = lax.axis_size(REP)
    shards = yh_n * z_n * x_n
    rep_index = lax.axis_index(REP)
    yh_index = lax.axis_index("yh")
    blocks = tile_blocks[0, 0]
    block_yh = blocks // (z_n * x_n)
    block_z = (blocks // x_n) % z_n
    places = (blocks % x_n) * (z_n * yh_n) + block_z * yh_n + block_yh
    panel = dense_panel(places, tile_counts[0, 0], tile_values[0, 0], shards)

    with jax.named_scope("gather_zy"):
        near = gather(features, ("z", "yh")).reshape(-1, width)
    with jax.named_scope("gather_x"):
        sources = gather(near, "x").reshape(shards * rows_dev, width)
    partial = lax.dot_general(
        panel, sources, (((0,), (0,)), ((), ())), preferred_element_type=f32
    )
    with jax.named_scope("panel_sum"):
        parts = exchange(partial.reshape(rep_n, rows_dev, width), REP)
        aggregate = jnp.sum(parts, axis=0).astype(bf16)
    preact = jnp.dot(aggregate, weight, preferred_element_type=f32)
    sigmoid_value = jax.nn.sigmoid(preact)
    activations = (preact * sigmoid_value).astype(bf16)
    own = lax.dynamic_slice_in_dim(cotangent, rep_index * rows_dev, rows_dev, 0).astype(f32)
    slope = (own * sigmoid_value * (1.0 + preact * (1.0 - sigmoid_value))).astype(bf16)
    with jax.named_scope("gather_rep"):
        both = gather(jnp.stack([aggregate, slope]), REP)
    panel_aggregate = both[:, 0].reshape(rep_n * rows_dev, width)
    panel_slope = both[:, 1].reshape(rep_n * rows_dev, width)
    panel_back = lax.dot_general(
        panel_slope, weight, (((1,), (1,)), ((), ())), preferred_element_type=f32
    ).astype(bf16)
    weight_part = lax.dot_general(
        panel_aggregate, panel_slope, (((0,), (0,)), ((), ())), preferred_element_type=f32
    )
    share = width // rep_n
    weight_rows = lax.dynamic_slice_in_dim(weight_part, rep_index * share, share, 0).astype(bf16)
    contrib = jnp.dot(panel, panel_back, preferred_element_type=f32).astype(bf16)

    with jax.named_scope("sum_x"):
        to_x = jnp.concatenate(
            [
                contrib.reshape(x_n, -1, width),
                jnp.broadcast_to(weight_rows, (x_n, share, width)),
            ],
            axis=1,
        )
        from_x = jnp.sum(exchange(to_x, "x").astype(f32), axis=0).astype(bf16)
    with jax.named_scope("sum_z"):
        to_z = jnp.concatenate(
            [
                from_x[:-share].reshape(z_n, yh_n * rows_dev, width),
                jnp.broadcast_to(from_x[-share:], (z_n, share, width)),
            ],
            axis=1,
        )
        from_z = jnp.sum(exchange(to_z, "z").astype(f32), axis=0)
    halves = from_z[:-share].reshape(yh_n, rows_dev, width)
    with jax.named_scope("sum_y"):
        away = lax.dynamic_index_in_dim(halves, 1 - yh_index, 0, keepdims=False).astype(bf16)
        arrived = lax.ppermute(away, "yh", [(0, 1), (1, 0)])
    with jax.named_scope("gather_weight"):
        weight_all = gather(from_z[-share:].astype(bf16), ("yh",) + REP)
        weight_all = weight_all.reshape(yh_n, width, width).astype(f32)
    here = lax.dynamic_index_in_dim(halves, yh_index, 0, keepdims=False)
    grad_features = (here + arrived.astype(f32)).astype(bf16)
    node_total = rows_dev * shards * rep_n
    grad_weight = jnp.sum(weight_all, axis=0) * float(node_total) ** (-0.5)
    return activations, grad_features, grad_weight


def solution(mesh):
    split = Mesh(mesh.devices.reshape(tuple(SPLIT.values())), tuple(SPLIT))
    return jax.shard_map(
        body,
        mesh=split,
        in_specs=(
            P(BLK + REP, None),
            P(),
            P(BLK, None),
            P(BLK, REP, None, None, None, None),
            P(BLK, REP, None, None),
            P(BLK, REP, None, None),
        ),
        out_specs=(P(BLK + REP, None), P(BLK + REP, None), P()),
        check_vma=False,
    )
```

```python
import jax
import jax.numpy as jnp
from jax import lax
from jax.experimental import pallas as pl
from jax.experimental.pallas import tpu as pltpu
from jax.sharding import Mesh, PartitionSpec as P

SPLIT = {"yh": 2, "zh": 4, "zl": 4, "x": 4, "yl": 4, "c": 2}
BLK = ("yh", "zh", "zl", "x")
FAR = ("zh", "yh")
NEAR = ("zl", "x")
REP = ("yl", "c")
bf16 = jnp.bfloat16
f32 = jnp.float32


def exchange(chunks, axes):
    return lax.all_to_all(chunks, axes, 0, 0, tiled=True)


def gather(block, axes):
    members = lax.axis_size(axes)
    return exchange(jnp.broadcast_to(block, (members,) + block.shape), axes)


def total(parts):
    return jnp.sum(parts.astype(f32), axis=0).astype(bf16)


def panel_kernel(places_ref, counts_ref, tiles_ref, panel_ref):
    row_tiles, slot_count, rows, tile_size = tiles_ref.shape
    total = panel_ref.shape[0]
    step = min(total, 256)

    def clear(i, carry):
        start = pl.multiple_of(i * step, step)
        panel_ref[pl.ds(start, step), :] = jnp.zeros((step, panel_ref.shape[1]), bf16)
        return carry

    lax.fori_loop(0, total // step, clear, 0)
    columns = lax.broadcasted_iota(jnp.int32, (rows, tile_size), 0)

    def place(slot, carry):
        for n in range(row_tiles):
            start = pl.multiple_of(places_ref[n, slot] * rows, rows)
            tile = tiles_ref[n, slot].astype(f32)
            kept = jnp.where(columns < counts_ref[n, slot], tile, 0.0).astype(bf16)
            panel_ref[pl.ds(start, rows), n * tile_size : (n + 1) * tile_size] = kept
        return carry

    lax.fori_loop(0, slot_count, place, 0, unroll=8)


def dense_panel(places, counts, tiles, blocks_total):
    row_tiles, _, rows, tile_size = tiles.shape
    return pl.pallas_call(
        panel_kernel,
        out_shape=jax.ShapeDtypeStruct((blocks_total * rows, row_tiles * tile_size), bf16),
        in_specs=[
            pl.BlockSpec(memory_space=pltpu.SMEM),
            pl.BlockSpec(memory_space=pltpu.SMEM),
            pl.BlockSpec(memory_space=pltpu.VMEM),
        ],
        out_specs=pl.BlockSpec(memory_space=pltpu.VMEM),
        compiler_params=pltpu.CompilerParams(vmem_limit_bytes=16 * 1024 * 1024),
        cost_estimate=pl.CostEstimate(flops=0, bytes_accessed=4 * 1024 * 1024, transcendentals=0),
    )(places, counts, tiles)


def body(features, weight, cotangent, tile_values, tile_counts, tile_blocks):
    rows_dev, width = features.shape
    yh_n, zh_n, zl_n, x_n = (lax.axis_size(a) for a in BLK)
    rep_n = lax.axis_size(REP)
    shards = yh_n * zh_n * zl_n * x_n
    rep_index = lax.axis_index(REP)
    blocks = tile_blocks[0, 0]
    block_x, block_zl = blocks % x_n, (blocks // x_n) % zl_n
    block_zh, block_yh = (blocks // (x_n * zl_n)) % zh_n, blocks // (x_n * zl_n * zh_n)
    places = ((block_x * zl_n + block_zl) * zh_n + block_zh) * yh_n + block_yh
    panel = dense_panel(places, tile_counts[0, 0], tile_values[0, 0], shards)

    with jax.named_scope("gather_far"):
        far = gather(features, FAR).reshape(-1, width)
    with jax.named_scope("gather_zl"):
        near = gather(far, "zl").reshape(-1, width)
    with jax.named_scope("gather_x"):
        sources = gather(near, "x").reshape(shards * rows_dev, width)
    partial = lax.dot_general(
        panel, sources, (((0,), (0,)), ((), ())), preferred_element_type=f32
    )
    with jax.named_scope("panel_sum"):
        parts = exchange(partial.reshape(rep_n, rows_dev, width), REP)
        aggregate = jnp.sum(parts, axis=0).astype(bf16)
    preact = jnp.dot(aggregate, weight, preferred_element_type=f32)
    sigmoid_value = jax.nn.sigmoid(preact)
    activations = (preact * sigmoid_value).astype(bf16)
    own = lax.dynamic_slice_in_dim(cotangent, rep_index * rows_dev, rows_dev, 0).astype(f32)
    slope = (own * sigmoid_value * (1.0 + preact * (1.0 - sigmoid_value))).astype(bf16)
    with jax.named_scope("gather_rep"):
        both = gather(jnp.stack([aggregate, slope]), REP)
    panel_aggregate = both[:, 0].reshape(rep_n * rows_dev, width)
    panel_slope = both[:, 1].reshape(rep_n * rows_dev, width)
    panel_back = lax.dot_general(
        panel_slope, weight, (((1,), (1,)), ((), ())), preferred_element_type=f32
    ).astype(bf16)
    weight_part = lax.dot_general(
        panel_aggregate, panel_slope, (((0,), (0,)), ((), ())), preferred_element_type=f32
    )
    share = width // rep_n
    weight_rows = lax.dynamic_slice_in_dim(weight_part, rep_index * share, share, 0).astype(bf16)
    contrib = jnp.dot(panel, panel_back, preferred_element_type=f32).astype(bf16)

    with jax.named_scope("sum_x"):
        from_x = lax.psum_scatter(contrib, "x", scatter_dimension=0, tiled=True)
    with jax.named_scope("weight_near"):
        weight_near = total(gather(weight_rows, NEAR))
    with jax.named_scope("sum_zl"):
        from_zl = total(exchange(from_x.reshape(zl_n, -1, width), "zl"))
    with jax.named_scope("sum_far"):
        far_parts = from_zl.reshape(zh_n * yh_n, rows_dev, width)
        weight_parts = jnp.broadcast_to(weight_near, (zh_n * yh_n,) + weight_near.shape)
        summed = total(exchange(jnp.concatenate([far_parts, weight_parts], axis=1), FAR))
        grad_features, weight_far = summed[:rows_dev], summed[rows_dev:]
    with jax.named_scope("weight_rep"):
        weight_all = gather(weight_far, REP).reshape(width, width).astype(f32)
    node_total = rows_dev * shards * rep_n
    return activations, grad_features, weight_all * float(node_total) ** (-0.5)


def solution(mesh):
    split = Mesh(mesh.devices.reshape(tuple(SPLIT.values())), tuple(SPLIT))
    return jax.shard_map(
        body,
        mesh=split,
        in_specs=(
            P(BLK + REP, None),
            P(),
            P(BLK, None),
            P(BLK, REP, None, None, None, None),
            P(BLK, REP, None, None),
            P(BLK, REP, None, None),
        ),
        out_specs=(P(BLK + REP, None), P(BLK + REP, None), P()),
        check_vma=False,
    )
```

```python
import jax
import jax.numpy as jnp
from jax import lax
from jax.experimental import pallas as pl
from jax.experimental.pallas import tpu as pltpu
from jax.sharding import Mesh, PartitionSpec as P

SPLIT = {"yh": 2, "zh": 4, "zl": 4, "x": 4, "yl": 4, "c": 2}
BLK = ("yh", "zh", "zl", "x")
FAR = ("zh", "yh")
REP = ("yl", "c")
bf16 = jnp.bfloat16
f32 = jnp.float32


def exchange(chunks, axes):
    return lax.all_to_all(chunks, axes, 0, 0, tiled=True)


def gather(block, axes):
    members = lax.axis_size(axes)
    return exchange(jnp.broadcast_to(block, (members,) + block.shape), axes)


def pairwise_sum(value, axis):
    members = lax.axis_size(axis)
    stride = 1
    while stride < members:
        pairs = [(i, i ^ stride) for i in range(members)]
        value = value + lax.ppermute(value, axis, pairs)
        stride *= 2
    return value


def total(parts):
    return jnp.sum(parts.astype(f32), axis=0).astype(bf16)


def panel_kernel(places_ref, counts_ref, tiles_ref, panel_ref):
    row_tiles, slot_count, rows, tile_size = tiles_ref.shape
    total = panel_ref.shape[0]
    step = min(total, 256)

    def clear(i, carry):
        start = pl.multiple_of(i * step, step)
        panel_ref[pl.ds(start, step), :] = jnp.zeros((step, panel_ref.shape[1]), bf16)
        return carry

    lax.fori_loop(0, total // step, clear, 0)
    columns = lax.broadcasted_iota(jnp.int32, (rows, tile_size), 0)

    def place(slot, carry):
        for n in range(row_tiles):
            start = pl.multiple_of(places_ref[n, slot] * rows, rows)
            tile = tiles_ref[n, slot].astype(f32)
            kept = jnp.where(columns < counts_ref[n, slot], tile, 0.0).astype(bf16)
            panel_ref[pl.ds(start, rows), n * tile_size : (n + 1) * tile_size] = kept
        return carry

    lax.fori_loop(0, slot_count, place, 0, unroll=8)


def dense_panel(places, counts, tiles, blocks_total):
    row_tiles, _, rows, tile_size = tiles.shape
    return pl.pallas_call(
        panel_kernel,
        out_shape=jax.ShapeDtypeStruct((blocks_total * rows, row_tiles * tile_size), bf16),
        in_specs=[
            pl.BlockSpec(memory_space=pltpu.SMEM),
            pl.BlockSpec(memory_space=pltpu.SMEM),
            pl.BlockSpec(memory_space=pltpu.VMEM),
        ],
        out_specs=pl.BlockSpec(memory_space=pltpu.VMEM),
        compiler_params=pltpu.CompilerParams(vmem_limit_bytes=16 * 1024 * 1024),
        cost_estimate=pl.CostEstimate(flops=0, bytes_accessed=4 * 1024 * 1024, transcendentals=0),
    )(places, counts, tiles)


def body(features, weight, cotangent, tile_values, tile_counts, tile_blocks):
    rows_dev, width = features.shape
    yh_n, zh_n, zl_n, x_n = (lax.axis_size(a) for a in BLK)
    rep_n = lax.axis_size(REP)
    shards = yh_n * zh_n * zl_n * x_n
    rep_index = lax.axis_index(REP)
    yh_index = lax.axis_index("yh")
    blocks = tile_blocks[0, 0]
    block_x, block_zl = blocks % x_n, (blocks // x_n) % zl_n
    block_zh, block_yh = (blocks // (x_n * zl_n)) % zh_n, blocks // (x_n * zl_n * zh_n)
    places = ((block_x * zl_n + block_zl) * zh_n + block_zh) * yh_n + block_yh
    panel = dense_panel(places, tile_counts[0, 0], tile_values[0, 0], shards)

    with jax.named_scope("gather_far"):
        far = gather(features, FAR).reshape(-1, width)
    with jax.named_scope("gather_zl"):
        near = gather(far, "zl").reshape(-1, width)
    with jax.named_scope("gather_x"):
        sources = gather(near, "x").reshape(shards * rows_dev, width)
    partial = lax.dot_general(
        panel, sources, (((0,), (0,)), ((), ())), preferred_element_type=f32
    )
    with jax.named_scope("panel_sum"):
        parts = exchange(partial.reshape(rep_n, rows_dev, width), REP)
        aggregate = jnp.sum(parts, axis=0).astype(bf16)
    preact = jnp.dot(aggregate, weight, preferred_element_type=f32)
    sigmoid_value = jax.nn.sigmoid(preact)
    activations = (preact * sigmoid_value).astype(bf16)
    own = lax.dynamic_slice_in_dim(cotangent, rep_index * rows_dev, rows_dev, 0).astype(f32)
    slope = (own * sigmoid_value * (1.0 + preact * (1.0 - sigmoid_value))).astype(bf16)
    with jax.named_scope("gather_rep"):
        both = gather(jnp.stack([aggregate, slope]), REP)
    panel_aggregate = both[:, 0].reshape(rep_n * rows_dev, width)
    panel_slope = both[:, 1].reshape(rep_n * rows_dev, width)
    panel_back = lax.dot_general(
        panel_slope, weight, (((1,), (1,)), ((), ())), preferred_element_type=f32
    ).astype(bf16)
    weight_part = lax.dot_general(
        panel_aggregate, panel_slope, (((0,), (0,)), ((), ())), preferred_element_type=f32
    )
    share = width // rep_n
    weight_rows = lax.dynamic_slice_in_dim(weight_part, rep_index * share, share, 0)
    contrib = jnp.dot(panel, panel_back, preferred_element_type=f32).astype(bf16)

    with jax.named_scope("sum_x"):
        parts = exchange(contrib.reshape(x_n, -1, width), "x")
        weight_rows = pairwise_sum(pairwise_sum(weight_rows, "x"), "zl")
        parts, weight_rows = lax.optimization_barrier((parts, weight_rows))
        from_x = total(parts)
    with jax.named_scope("sum_zl"):
        parts = exchange(from_x.reshape(zl_n, -1, width), "zl")
        weight_rows = pairwise_sum(weight_rows, "zh")
        parts, weight_rows = lax.optimization_barrier((parts, weight_rows))
        from_zl = total(parts)
    with jax.named_scope("sum_zh"):
        parts = exchange(from_zl.reshape(zh_n, yh_n * rows_dev, width), "zh")
        weight_rows = pairwise_sum(weight_rows, "yh")
        parts, weight_rows = lax.optimization_barrier((parts, weight_rows))
        halves = jnp.sum(parts.astype(f32), axis=0).reshape(yh_n, rows_dev, width)
    with jax.named_scope("sum_yh"):
        away = lax.dynamic_index_in_dim(halves, 1 - yh_index, 0, keepdims=False).astype(bf16)
        here = lax.dynamic_index_in_dim(halves, yh_index, 0, keepdims=False)
        arrived = lax.ppermute(away, "yh", [(0, 1), (1, 0)])
        grad_features = (here + arrived.astype(f32)).astype(bf16)
    with jax.named_scope("weight_rep"):
        weight_all = gather(weight_rows.astype(bf16), REP).reshape(width, width).astype(f32)
    node_total = rows_dev * shards * rep_n
    return activations, grad_features, weight_all * float(node_total) ** (-0.5)


def solution(mesh):
    split = Mesh(mesh.devices.reshape(tuple(SPLIT.values())), tuple(SPLIT))
    return jax.shard_map(
        body,
        mesh=split,
        in_specs=(
            P(BLK + REP, None),
            P(),
            P(BLK, None),
            P(BLK, REP, None, None, None, None),
            P(BLK, REP, None, None),
            P(BLK, REP, None, None),
        ),
        out_specs=(P(BLK + REP, None), P(BLK + REP, None), P()),
        check_vma=False,
    )
```

```python
import jax
import jax.numpy as jnp
from jax import lax
from jax.experimental import pallas as pl
from jax.experimental.pallas import tpu as pltpu
from jax.sharding import Mesh, PartitionSpec as P

SPLIT = {"yh": 2, "z": 16, "x": 4, "yl": 4, "c": 2}
BLK = ("yh", "z", "x")
REP = ("yl", "c")
bf16 = jnp.bfloat16
f32 = jnp.float32


def exchange(chunks, axes):
    return lax.all_to_all(chunks, axes, 0, 0, tiled=True)


def gather(block, axes):
    members = lax.axis_size(axes)
    return exchange(jnp.broadcast_to(block, (members,) + block.shape), axes)


def pairwise_sum(value, axis):
    members = lax.axis_size(axis)
    stride = 1
    while stride < members:
        pairs = [(i, i ^ stride) for i in range(members)]
        value = value + lax.ppermute(value, axis, pairs)
        stride *= 2
    return value


def panel_kernel(places_ref, counts_ref, tiles_ref, panel_ref):
    row_tiles, slot_count, rows, tile_size = tiles_ref.shape
    total = panel_ref.shape[0]
    step = min(total, 256)

    def clear(i, carry):
        start = pl.multiple_of(i * step, step)
        panel_ref[pl.ds(start, step), :] = jnp.zeros((step, panel_ref.shape[1]), bf16)
        return carry

    lax.fori_loop(0, total // step, clear, 0)
    columns = lax.broadcasted_iota(jnp.int32, (rows, tile_size), 0)

    def place(slot, carry):
        for n in range(row_tiles):
            start = pl.multiple_of(places_ref[n, slot] * rows, rows)
            tile = tiles_ref[n, slot].astype(f32)
            kept = jnp.where(columns < counts_ref[n, slot], tile, 0.0).astype(bf16)
            panel_ref[pl.ds(start, rows), n * tile_size : (n + 1) * tile_size] = kept
        return carry

    lax.fori_loop(0, slot_count, place, 0, unroll=8)


def dense_panel(places, counts, tiles, blocks_total):
    row_tiles, _, rows, tile_size = tiles.shape
    return pl.pallas_call(
        panel_kernel,
        out_shape=jax.ShapeDtypeStruct((blocks_total * rows, row_tiles * tile_size), bf16),
        in_specs=[
            pl.BlockSpec(memory_space=pltpu.SMEM),
            pl.BlockSpec(memory_space=pltpu.SMEM),
            pl.BlockSpec(memory_space=pltpu.VMEM),
        ],
        out_specs=pl.BlockSpec(memory_space=pltpu.VMEM),
        compiler_params=pltpu.CompilerParams(vmem_limit_bytes=16 * 1024 * 1024),
        cost_estimate=pl.CostEstimate(flops=0, bytes_accessed=4 * 1024 * 1024, transcendentals=0),
    )(places, counts, tiles)


def body(features, weight, cotangent, tile_values, tile_counts, tile_blocks):
    rows_dev, width = features.shape
    yh_n, z_n, x_n = (lax.axis_size(a) for a in BLK)
    rep_n = lax.axis_size(REP)
    shards = yh_n * z_n * x_n
    rep_index = lax.axis_index(REP)
    yh_index = lax.axis_index("yh")
    blocks = tile_blocks[0, 0]
    block_yh = blocks // (z_n * x_n)
    block_z = (blocks // x_n) % z_n
    places = (blocks % x_n) * (z_n * yh_n) + block_z * yh_n + block_yh
    panel = dense_panel(places, tile_counts[0, 0], tile_values[0, 0], shards)

    with jax.named_scope("gather_zy"):
        near = gather(features, ("z", "yh")).reshape(-1, width)
    with jax.named_scope("gather_x"):
        sources = gather(near, "x").reshape(shards * rows_dev, width)
    partial = lax.dot_general(
        panel, sources, (((0,), (0,)), ((), ())), preferred_element_type=f32
    )
    with jax.named_scope("panel_sum"):
        parts = exchange(partial.reshape(rep_n, rows_dev, width), REP)
        aggregate = jnp.sum(parts, axis=0).astype(bf16)
    preact = jnp.dot(aggregate, weight, preferred_element_type=f32)
    sigmoid_value = jax.nn.sigmoid(preact)
    activations = (preact * sigmoid_value).astype(bf16)
    own = lax.dynamic_slice_in_dim(cotangent, rep_index * rows_dev, rows_dev, 0).astype(f32)
    slope = (own * sigmoid_value * (1.0 + preact * (1.0 - sigmoid_value))).astype(bf16)
    with jax.named_scope("gather_rep"):
        both = gather(jnp.stack([aggregate, slope]), REP)
    panel_aggregate = both[:, 0].reshape(rep_n * rows_dev, width)
    panel_slope = both[:, 1].reshape(rep_n * rows_dev, width)
    panel_back = lax.dot_general(
        panel_slope, weight, (((1,), (1,)), ((), ())), preferred_element_type=f32
    ).astype(bf16)
    weight_part = lax.dot_general(
        panel_aggregate, panel_slope, (((0,), (0,)), ((), ())), preferred_element_type=f32
    )
    share = width // rep_n
    weight_rows = lax.dynamic_slice_in_dim(weight_part, rep_index * share, share, 0)
    contrib = jnp.dot(panel, panel_back, preferred_element_type=f32).astype(bf16)

    with jax.named_scope("sum_x"):
        parts = exchange(contrib.reshape(x_n, -1, width), "x")
        weight_rows = pairwise_sum(weight_rows, "z")
        parts, weight_rows = lax.optimization_barrier((parts, weight_rows))
        from_x = jnp.sum(parts.astype(f32), axis=0).astype(bf16)
    with jax.named_scope("sum_z"):
        parts = exchange(from_x.reshape(z_n, -1, width), "z")
        weight_rows = pairwise_sum(pairwise_sum(weight_rows, "x"), "yh")
        parts, weight_rows = lax.optimization_barrier((parts, weight_rows))
        halves = jnp.sum(parts.astype(f32), axis=0).reshape(yh_n, rows_dev, width)
    with jax.named_scope("sum_y"):
        away = lax.dynamic_index_in_dim(halves, 1 - yh_index, 0, keepdims=False).astype(bf16)
        here = lax.dynamic_index_in_dim(halves, yh_index, 0, keepdims=False)
        arrived = lax.ppermute(away, "yh", [(0, 1), (1, 0)])
        grad_features = (here + arrived.astype(f32)).astype(bf16)
    with jax.named_scope("weight_rep"):
        weight_all = gather(weight_rows.astype(bf16), REP).reshape(width, width).astype(f32)
    node_total = rows_dev * shards * rep_n
    grad_weight = weight_all * float(node_total) ** (-0.5)
    return activations, grad_features, grad_weight


def solution(mesh):
    split = Mesh(mesh.devices.reshape(tuple(SPLIT.values())), tuple(SPLIT))
    return jax.shard_map(
        body,
        mesh=split,
        in_specs=(
            P(BLK + REP, None),
            P(),
            P(BLK, None),
            P(BLK, REP, None, None, None, None),
            P(BLK, REP, None, None),
            P(BLK, REP, None, None),
        ),
        out_specs=(P(BLK + REP, None), P(BLK + REP, None), P()),
        check_vma=False,
    )
```

```python
import jax
import jax.numpy as jnp
from jax import lax
from jax.experimental import pallas as pl
from jax.experimental.pallas import tpu as pltpu
from jax.sharding import Mesh, PartitionSpec as P

SPLIT = {"yh": 2, "z": 16, "x": 4, "yl": 4, "c": 2}
BLK = ("yh", "z", "x")
REP = ("yl", "c")
bf16 = jnp.bfloat16
f32 = jnp.float32


def exchange(chunks, axes):
    return lax.all_to_all(chunks, axes, 0, 0, tiled=True)


def gather(block, axes):
    members = lax.axis_size(axes)
    return exchange(jnp.broadcast_to(block, (members,) + block.shape), axes)


def from_ahead(value, axis):
    members = lax.axis_size(axis)
    return lax.ppermute(value, axis, [(i, (i - 1) % members) for i in range(members)])


def from_behind(value, axis):
    members = lax.axis_size(axis)
    return lax.ppermute(value, axis, [(i, (i + 1) % members) for i in range(members)])


def pairwise_sum(value, axis, members):
    stride = 1
    while stride < members:
        pairs = [(i, i ^ stride) for i in range(lax.axis_size(axis))]
        value = value + lax.ppermute(value, axis, pairs)
        stride *= 2
    return value


def mirror_sum(value, axis):
    members = lax.axis_size(axis)
    return value + lax.ppermute(value, axis, [(i, members - 1 - i) for i in range(members)])


def panel_kernel(places_ref, counts_ref, tiles_ref, panel_ref):
    row_tiles, slot_count, rows, tile_size = tiles_ref.shape
    total = panel_ref.shape[0]
    step = min(total, 256)

    def clear(i, carry):
        start = pl.multiple_of(i * step, step)
        panel_ref[pl.ds(start, step), :] = jnp.zeros((step, panel_ref.shape[1]), bf16)
        return carry

    lax.fori_loop(0, total // step, clear, 0)
    columns = lax.broadcasted_iota(jnp.int32, (rows, tile_size), 0)

    def place(slot, carry):
        for n in range(row_tiles):
            start = pl.multiple_of(places_ref[n, slot] * rows, rows)
            tile = tiles_ref[n, slot].astype(f32)
            kept = jnp.where(columns < counts_ref[n, slot], tile, 0.0).astype(bf16)
            panel_ref[pl.ds(start, rows), n * tile_size : (n + 1) * tile_size] = kept
        return carry

    lax.fori_loop(0, slot_count, place, 0, unroll=8)


def dense_panel(places, counts, tiles, blocks_total):
    row_tiles, _, rows, tile_size = tiles.shape
    return pl.pallas_call(
        panel_kernel,
        out_shape=jax.ShapeDtypeStruct((blocks_total * rows, row_tiles * tile_size), bf16),
        in_specs=[
            pl.BlockSpec(memory_space=pltpu.SMEM),
            pl.BlockSpec(memory_space=pltpu.SMEM),
            pl.BlockSpec(memory_space=pltpu.VMEM),
        ],
        out_specs=pl.BlockSpec(memory_space=pltpu.VMEM),
        compiler_params=pltpu.CompilerParams(vmem_limit_bytes=16 * 1024 * 1024),
        cost_estimate=pl.CostEstimate(flops=0, bytes_accessed=4 * 1024 * 1024, transcendentals=0),
    )(places, counts, tiles)


def body(features, weight, cotangent, tile_values, tile_counts, tile_blocks):
    rows_dev, width = features.shape
    yh_n, z_n, x_n = (lax.axis_size(a) for a in BLK)
    rep_n = lax.axis_size(REP)
    shards = yh_n * z_n * x_n
    rep_index = lax.axis_index(REP)
    x_index = lax.axis_index("x")
    blocks = tile_blocks[0, 0]
    block_yh = blocks // (z_n * x_n)
    block_z = (blocks // x_n) % z_n
    block_x = (blocks % x_n - x_index + x_n) % x_n
    places = (block_x * z_n + block_z) * yh_n + block_yh
    panel = dense_panel(places, tile_counts[0, 0], tile_values[0, 0], shards)

    with jax.named_scope("gather_zy"):
        near = gather(features, ("z", "yh")).reshape(-1, width)
    section = near.shape[0]
    half = section // 2

    def product(start, values):
        return lax.dot_general(
            panel[start : start + values.shape[0]],
            values,
            (((0,), (0,)), ((), ())),
            preferred_element_type=f32,
        )

    with jax.named_scope("gather_x"):
        ahead = from_ahead(near, "x")
        behind = from_behind(near, "x")
        far_top = from_ahead(ahead[:half], "x")
        far_bottom = from_behind(behind[half:], "x")
    partial = product(0, near) + product(section, ahead) + product(3 * section, behind)
    partial = partial + product(2 * section, far_top) + product(2 * section + half, far_bottom)
    with jax.named_scope("panel_sum"):
        parts = exchange(partial.reshape(rep_n, rows_dev, width), REP)
        aggregate = jnp.sum(parts, axis=0).astype(bf16)
    preact = jnp.dot(aggregate, weight, preferred_element_type=f32)
    sigmoid_value = jax.nn.sigmoid(preact)
    activations = (preact * sigmoid_value).astype(bf16)
    own = lax.dynamic_slice_in_dim(cotangent, rep_index * rows_dev, rows_dev, 0).astype(f32)
    slope = (own * sigmoid_value * (1.0 + preact * (1.0 - sigmoid_value))).astype(bf16)
    with jax.named_scope("gather_rep"):
        both = gather(jnp.stack([aggregate, slope]), REP)
    panel_aggregate = both[:, 0].reshape(rep_n * rows_dev, width)
    panel_slope = both[:, 1].reshape(rep_n * rows_dev, width)
    panel_back = lax.dot_general(
        panel_slope, weight, (((1,), (1,)), ((), ())), preferred_element_type=f32
    ).astype(bf16)
    weight_part = lax.dot_general(
        panel_aggregate, panel_slope, (((0,), (0,)), ((), ())), preferred_element_type=f32
    )
    share = width // rep_n
    weight_rows = lax.dynamic_slice_in_dim(weight_part, rep_index * share, share, 0)
    def share_of(k):
        return jnp.dot(
            panel[k * section : (k + 1) * section], panel_back, preferred_element_type=f32
        )

    with jax.named_scope("sum_x"):
        far = share_of(2).astype(bf16)
        top = from_behind(far[:half], "x").astype(f32)
        bottom = from_ahead(far[half:], "x").astype(f32)
        right, left = share_of(1), share_of(3)
        right = jnp.concatenate([right[:half] + top, right[half:]]).astype(bf16)
        left = jnp.concatenate([left[:half], left[half:] + bottom]).astype(bf16)
        arrived = (from_behind(right, "x"), from_ahead(left, "x"))
        weight_rows = mirror_sum(pairwise_sum(weight_rows, "z", z_n // 2), "z")
        arrived, weight_rows = lax.optimization_barrier((arrived, weight_rows))
        from_x = (share_of(0) + arrived[0].astype(f32) + arrived[1].astype(f32)).astype(bf16)
    with jax.named_scope("sum_zy"):
        parts = exchange(from_x.reshape(-1, rows_dev, width), ("z", "yh"))
        weight_rows = pairwise_sum(pairwise_sum(weight_rows, "x", x_n), "yh", yh_n)
        parts, weight_rows = lax.optimization_barrier((parts, weight_rows))
        grad_features = jnp.sum(parts.astype(f32), axis=0).astype(bf16)
    with jax.named_scope("weight_rep"):
        weight_all = gather(weight_rows.astype(bf16), REP).reshape(width, width).astype(f32)
    node_total = rows_dev * shards * rep_n
    grad_weight = weight_all * float(node_total) ** (-0.5)
    return activations, grad_features, grad_weight


def solution(mesh):
    split = Mesh(mesh.devices.reshape(tuple(SPLIT.values())), tuple(SPLIT))
    return jax.shard_map(
        body,
        mesh=split,
        in_specs=(
            P(BLK + REP, None),
            P(),
            P(BLK, None),
            P(BLK, REP, None, None, None, None),
            P(BLK, REP, None, None),
            P(BLK, REP, None, None),
        ),
        out_specs=(P(BLK + REP, None), P(BLK + REP, None), P()),
        check_vma=False,
    )
```

```python
import jax
import jax.numpy as jnp
from jax import lax
from jax.experimental import pallas as pl
from jax.experimental.pallas import tpu as pltpu
from jax.sharding import Mesh, PartitionSpec as P

SPLIT = {"yh": 2, "z": 16, "x": 4, "yl": 4, "c": 2}
BLK = ("yh", "z", "x")
REP = ("yl", "c")
bf16 = jnp.bfloat16
f32 = jnp.float32


def exchange(chunks, axes):
    return lax.all_to_all(chunks, axes, 0, 0, tiled=True)


def gather(block, axes):
    members = lax.axis_size(axes)
    return exchange(jnp.broadcast_to(block, (members,) + block.shape), axes)


def from_ahead(value, axis):
    members = lax.axis_size(axis)
    return lax.ppermute(value, axis, [(i, (i - 1) % members) for i in range(members)])


def from_behind(value, axis):
    members = lax.axis_size(axis)
    return lax.ppermute(value, axis, [(i, (i + 1) % members) for i in range(members)])


def pairwise_sum(value, axis, members):
    stride = 1
    while stride < members:
        pairs = [(i, i ^ stride) for i in range(lax.axis_size(axis))]
        value = value + lax.ppermute(value, axis, pairs)
        stride *= 2
    return value


def panel_kernel(places_ref, counts_ref, tiles_ref, panel_ref):
    row_tiles, slot_count, rows, tile_size = tiles_ref.shape
    total = panel_ref.shape[0]
    step = min(total, 256)

    def clear(i, carry):
        start = pl.multiple_of(i * step, step)
        panel_ref[pl.ds(start, step), :] = jnp.zeros((step, panel_ref.shape[1]), bf16)
        return carry

    lax.fori_loop(0, total // step, clear, 0)
    columns = lax.broadcasted_iota(jnp.int32, (rows, tile_size), 0)

    def place(slot, carry):
        for n in range(row_tiles):
            start = pl.multiple_of(places_ref[n, slot] * rows, rows)
            tile = tiles_ref[n, slot].astype(f32)
            kept = jnp.where(columns < counts_ref[n, slot], tile, 0.0).astype(bf16)
            panel_ref[pl.ds(start, rows), n * tile_size : (n + 1) * tile_size] = kept
        return carry

    lax.fori_loop(0, slot_count, place, 0, unroll=8)


def dense_panel(places, counts, tiles, blocks_total):
    row_tiles, _, rows, tile_size = tiles.shape
    return pl.pallas_call(
        panel_kernel,
        out_shape=jax.ShapeDtypeStruct((blocks_total * rows, row_tiles * tile_size), bf16),
        in_specs=[
            pl.BlockSpec(memory_space=pltpu.SMEM),
            pl.BlockSpec(memory_space=pltpu.SMEM),
            pl.BlockSpec(memory_space=pltpu.VMEM),
        ],
        out_specs=pl.BlockSpec(memory_space=pltpu.VMEM),
        compiler_params=pltpu.CompilerParams(vmem_limit_bytes=16 * 1024 * 1024),
        cost_estimate=pl.CostEstimate(flops=0, bytes_accessed=4 * 1024 * 1024, transcendentals=0),
    )(places, counts, tiles)


def body(features, weight, cotangent, tile_values, tile_counts, tile_blocks):
    rows_dev, width = features.shape
    yh_n, z_n, x_n = (lax.axis_size(a) for a in BLK)
    rep_n = lax.axis_size(REP)
    shards = yh_n * z_n * x_n
    rep_index = lax.axis_index(REP)
    x_index = lax.axis_index("x")
    blocks = tile_blocks[0, 0]
    block_yh = blocks // (z_n * x_n)
    block_z = (blocks // x_n) % z_n
    block_x = (blocks % x_n - x_index + x_n) % x_n
    places = (block_x * z_n + block_z) * yh_n + block_yh
    panel = dense_panel(places, tile_counts[0, 0], tile_values[0, 0], shards)

    with jax.named_scope("gather_zy"):
        near = gather(features, ("z", "yh")).reshape(-1, width)
    section = near.shape[0]
    half = section // 2

    def product(start, values):
        return lax.dot_general(
            panel[start : start + values.shape[0]],
            values,
            (((0,), (0,)), ((), ())),
            preferred_element_type=f32,
        )

    with jax.named_scope("gather_x"):
        ahead = from_ahead(near, "x")
        behind = from_behind(near, "x")
        far_top = from_ahead(ahead[:half], "x")
        far_bottom = from_behind(behind[half:], "x")
    partial = product(0, near) + product(section, ahead) + product(3 * section, behind)
    partial = partial + product(2 * section, far_top) + product(2 * section + half, far_bottom)
    with jax.named_scope("panel_sum"):
        parts = exchange(partial.reshape(rep_n, rows_dev, width), REP)
        aggregate = jnp.sum(parts, axis=0).astype(bf16)
    preact = jnp.dot(aggregate, weight, preferred_element_type=f32)
    sigmoid_value = jax.nn.sigmoid(preact)
    activations = (preact * sigmoid_value).astype(bf16)
    own = lax.dynamic_slice_in_dim(cotangent, rep_index * rows_dev, rows_dev, 0).astype(f32)
    slope = (own * sigmoid_value * (1.0 + preact * (1.0 - sigmoid_value))).astype(bf16)
    with jax.named_scope("gather_rep"):
        both = gather(jnp.stack([aggregate, slope]), REP)
    panel_aggregate = both[:, 0].reshape(rep_n * rows_dev, width)
    panel_slope = both[:, 1].reshape(rep_n * rows_dev, width)
    panel_back = lax.dot_general(
        panel_slope, weight, (((1,), (1,)), ((), ())), preferred_element_type=f32
    ).astype(bf16)
    weight_part = lax.dot_general(
        panel_aggregate, panel_slope, (((0,), (0,)), ((), ())), preferred_element_type=f32
    )
    share = width // rep_n
    weight_rows = lax.dynamic_slice_in_dim(weight_part, rep_index * share, share, 0)
    def share_of(k):
        return jnp.dot(
            panel[k * section : (k + 1) * section], panel_back, preferred_element_type=f32
        )

    with jax.named_scope("sum_x"):
        far = share_of(2).astype(bf16)
        top = from_behind(far[:half], "x").astype(f32)
        bottom = from_ahead(far[half:], "x").astype(f32)
        right, left = share_of(1), share_of(3)
        right = jnp.concatenate([right[:half] + top, right[half:]]).astype(bf16)
        left = jnp.concatenate([left[:half], left[half:] + bottom]).astype(bf16)
        arrived = (from_behind(right, "x"), from_ahead(left, "x"))
        weight_rows = jnp.sum(gather(weight_rows.astype(bf16), "z").astype(f32), axis=0)
        arrived, weight_rows = lax.optimization_barrier((arrived, weight_rows))
        from_x = (share_of(0) + arrived[0].astype(f32) + arrived[1].astype(f32)).astype(bf16)
    with jax.named_scope("sum_zy"):
        parts = exchange(from_x.reshape(-1, rows_dev, width), ("z", "yh"))
        weight_rows = pairwise_sum(pairwise_sum(weight_rows, "x", x_n), "yh", yh_n)
        parts, weight_rows = lax.optimization_barrier((parts, weight_rows))
        grad_features = jnp.sum(parts.astype(f32), axis=0).astype(bf16)
    with jax.named_scope("weight_rep"):
        weight_all = gather(weight_rows.astype(bf16), REP).reshape(width, width).astype(f32)
    node_total = rows_dev * shards * rep_n
    grad_weight = weight_all * float(node_total) ** (-0.5)
    return activations, grad_features, grad_weight


def solution(mesh):
    split = Mesh(mesh.devices.reshape(tuple(SPLIT.values())), tuple(SPLIT))
    return jax.shard_map(
        body,
        mesh=split,
        in_specs=(
            P(BLK + REP, None),
            P(),
            P(BLK, None),
            P(BLK, REP, None, None, None, None),
            P(BLK, REP, None, None),
            P(BLK, REP, None, None),
        ),
        out_specs=(P(BLK + REP, None), P(BLK + REP, None), P()),
        check_vma=False,
    )
```

```python
import jax
import jax.numpy as jnp
from jax import lax
from jax.experimental import pallas as pl
from jax.experimental.pallas import tpu as pltpu
from jax.sharding import Mesh, PartitionSpec as P

SPLIT = {"yh": 2, "z": 16, "x": 4, "yl": 4, "c": 2}
BLK = ("yh", "z", "x")
REP = ("yl", "c")
bf16 = jnp.bfloat16
f32 = jnp.float32


def exchange(chunks, axes):
    return lax.all_to_all(chunks, axes, 0, 0, tiled=True)


def gather(block, axes):
    members = lax.axis_size(axes)
    return exchange(jnp.broadcast_to(block, (members,) + block.shape), axes)


def from_ahead(value, axis):
    members = lax.axis_size(axis)
    return lax.ppermute(value, axis, [(i, (i - 1) % members) for i in range(members)])


def from_behind(value, axis):
    members = lax.axis_size(axis)
    return lax.ppermute(value, axis, [(i, (i + 1) % members) for i in range(members)])


def pairwise_sum(value, axis, members):
    stride = 1
    while stride < members:
        pairs = [(i, i ^ stride) for i in range(lax.axis_size(axis))]
        value = value + lax.ppermute(value, axis, pairs)
        stride *= 2
    return value


def mirror_sum(value, axis):
    members = lax.axis_size(axis)
    return value + lax.ppermute(value, axis, [(i, members - 1 - i) for i in range(members)])


def panel_kernel(places_ref, counts_ref, tiles_ref, panel_ref):
    row_tiles, slot_count, rows, tile_size = tiles_ref.shape
    total = panel_ref.shape[0]
    step = min(total, 256)

    def clear(i, carry):
        start = pl.multiple_of(i * step, step)
        panel_ref[pl.ds(start, step), :] = jnp.zeros((step, panel_ref.shape[1]), bf16)
        return carry

    lax.fori_loop(0, total // step, clear, 0)
    columns = lax.broadcasted_iota(jnp.int32, (rows, tile_size), 0)

    def place(slot, carry):
        for n in range(row_tiles):
            start = pl.multiple_of(places_ref[n, slot] * rows, rows)
            tile = tiles_ref[n, slot].astype(f32)
            kept = jnp.where(columns < counts_ref[n, slot], tile, 0.0).astype(bf16)
            panel_ref[pl.ds(start, rows), n * tile_size : (n + 1) * tile_size] = kept
        return carry

    lax.fori_loop(0, slot_count, place, 0, unroll=8)


def dense_panel(places, counts, tiles, blocks_total):
    row_tiles, _, rows, tile_size = tiles.shape
    return pl.pallas_call(
        panel_kernel,
        out_shape=jax.ShapeDtypeStruct((blocks_total * rows, row_tiles * tile_size), bf16),
        in_specs=[
            pl.BlockSpec(memory_space=pltpu.SMEM),
            pl.BlockSpec(memory_space=pltpu.SMEM),
            pl.BlockSpec(memory_space=pltpu.VMEM),
        ],
        out_specs=pl.BlockSpec(memory_space=pltpu.VMEM),
        compiler_params=pltpu.CompilerParams(vmem_limit_bytes=16 * 1024 * 1024),
        cost_estimate=pl.CostEstimate(flops=0, bytes_accessed=4 * 1024 * 1024, transcendentals=0),
    )(places, counts, tiles)


def body(features, weight, cotangent, tile_values, tile_counts, tile_blocks):
    rows_dev, width = features.shape
    yh_n, z_n, x_n = (lax.axis_size(a) for a in BLK)
    rep_n = lax.axis_size(REP)
    shards = yh_n * z_n * x_n
    rep_index = lax.axis_index(REP)
    yh_index = lax.axis_index("yh")
    x_index = lax.axis_index("x")
    blocks = tile_blocks[0, 0]
    block_yh = blocks // (z_n * x_n)
    block_z = (blocks // x_n) % z_n
    places = (blocks % x_n) * (z_n * yh_n) + block_z * yh_n + block_yh
    panel = dense_panel(places, tile_counts[0, 0], tile_values[0, 0], shards)

    with jax.named_scope("gather_zy"):
        near = gather(features, ("z", "yh")).reshape(-1, width)
    section = near.shape[0]
    half = section // 2

    def product(distance, values, offset=0):
        start = ((x_index + distance) % x_n) * section + offset
        rows = lax.dynamic_slice_in_dim(panel, start, values.shape[0], 0)
        return lax.dot_general(
            rows, values, (((0,), (0,)), ((), ())), preferred_element_type=f32
        )

    with jax.named_scope("gather_x"):
        ahead = from_ahead(near, "x")
        behind = from_behind(near, "x")
        far_top = from_ahead(ahead[:half], "x")
        far_bottom = from_behind(behind[half:], "x")
    partial = product(0, near) + product(1, ahead) + product(3, behind)
    partial = partial + product(2, far_top) + product(2, far_bottom, half)
    with jax.named_scope("panel_sum"):
        parts = exchange(partial.reshape(rep_n, rows_dev, width), REP)
        aggregate = jnp.sum(parts, axis=0).astype(bf16)
    preact = jnp.dot(aggregate, weight, preferred_element_type=f32)
    sigmoid_value = jax.nn.sigmoid(preact)
    activations = (preact * sigmoid_value).astype(bf16)
    own = lax.dynamic_slice_in_dim(cotangent, rep_index * rows_dev, rows_dev, 0).astype(f32)
    slope = (own * sigmoid_value * (1.0 + preact * (1.0 - sigmoid_value))).astype(bf16)
    with jax.named_scope("gather_rep"):
        both = gather(jnp.stack([aggregate, slope]), REP)
    panel_aggregate = both[:, 0].reshape(rep_n * rows_dev, width)
    panel_slope = both[:, 1].reshape(rep_n * rows_dev, width)
    panel_back = lax.dot_general(
        panel_slope, weight, (((1,), (1,)), ((), ())), preferred_element_type=f32
    ).astype(bf16)
    weight_part = lax.dot_general(
        panel_aggregate, panel_slope, (((0,), (0,)), ((), ())), preferred_element_type=f32
    )
    share = width // rep_n
    weight_rows = lax.dynamic_slice_in_dim(weight_part, rep_index * share, share, 0)
    contrib = jnp.dot(panel, panel_back, preferred_element_type=f32).astype(bf16)

    with jax.named_scope("sum_x"):
        parts = exchange(contrib.reshape(x_n, -1, width), "x")
        weight_rows = mirror_sum(pairwise_sum(weight_rows, "z", z_n // 2), "z")
        parts, weight_rows = lax.optimization_barrier((parts, weight_rows))
        from_x = jnp.sum(parts.astype(f32), axis=0).astype(bf16)
    with jax.named_scope("sum_z"):
        parts = exchange(from_x.reshape(z_n, -1, width), "z")
        weight_rows = pairwise_sum(pairwise_sum(weight_rows, "x", x_n), "yh", yh_n)
        parts, weight_rows = lax.optimization_barrier((parts, weight_rows))
        halves = jnp.sum(parts.astype(f32), axis=0).reshape(yh_n, rows_dev, width)
    with jax.named_scope("sum_y"):
        away = lax.dynamic_index_in_dim(halves, 1 - yh_index, 0, keepdims=False).astype(bf16)
        here = lax.dynamic_index_in_dim(halves, yh_index, 0, keepdims=False)
        arrived = lax.ppermute(away, "yh", [(0, 1), (1, 0)])
        grad_features = (here + arrived.astype(f32)).astype(bf16)
    with jax.named_scope("weight_rep"):
        weight_all = gather(weight_rows.astype(bf16), REP).reshape(width, width).astype(f32)
    node_total = rows_dev * shards * rep_n
    grad_weight = weight_all * float(node_total) ** (-0.5)
    return activations, grad_features, grad_weight


def solution(mesh):
    split = Mesh(mesh.devices.reshape(tuple(SPLIT.values())), tuple(SPLIT))
    return jax.shard_map(
        body,
        mesh=split,
        in_specs=(
            P(BLK + REP, None),
            P(),
            P(BLK, None),
            P(BLK, REP, None, None, None, None),
            P(BLK, REP, None, None),
            P(BLK, REP, None, None),
        ),
        out_specs=(P(BLK + REP, None), P(BLK + REP, None), P()),
        check_vma=False,
    )
```

```python
import jax
import jax.numpy as jnp
from jax import lax
from jax.experimental import pallas as pl
from jax.experimental.pallas import tpu as pltpu
from jax.sharding import Mesh, PartitionSpec as P

SPLIT = {"yh": 2, "z": 16, "x": 4, "yl": 4, "c": 2}
BLK = ("yh", "z", "x")
REP = ("yl", "c")
bf16 = jnp.bfloat16
f32 = jnp.float32


def exchange(chunks, axes):
    return lax.all_to_all(chunks, axes, 0, 0, tiled=True)


def gather(block, axes):
    members = lax.axis_size(axes)
    return exchange(jnp.broadcast_to(block, (members,) + block.shape), axes)


def from_ahead(value, axis):
    members = lax.axis_size(axis)
    return lax.ppermute(value, axis, [(i, (i - 1) % members) for i in range(members)])


def from_behind(value, axis):
    members = lax.axis_size(axis)
    return lax.ppermute(value, axis, [(i, (i + 1) % members) for i in range(members)])


def pairwise_sum(value, axis, members):
    stride = 1
    while stride < members:
        pairs = [(i, i ^ stride) for i in range(lax.axis_size(axis))]
        value = value + lax.ppermute(value, axis, pairs)
        stride *= 2
    return value


def mirror_sum(value, axis):
    members = lax.axis_size(axis)
    return value + lax.ppermute(value, axis, [(i, members - 1 - i) for i in range(members)])


def panel_kernel(places_ref, counts_ref, tiles_ref, panel_ref):
    row_tiles, slot_count, rows, tile_size = tiles_ref.shape
    total = panel_ref.shape[0]
    step = min(total, 256)

    def clear(i, carry):
        start = pl.multiple_of(i * step, step)
        panel_ref[pl.ds(start, step), :] = jnp.zeros((step, panel_ref.shape[1]), bf16)
        return carry

    lax.fori_loop(0, total // step, clear, 0)
    columns = lax.broadcasted_iota(jnp.int32, (rows, tile_size), 0)

    def place(slot, carry):
        for n in range(row_tiles):
            start = pl.multiple_of(places_ref[n, slot] * rows, rows)
            tile = tiles_ref[n, slot].astype(f32)
            kept = jnp.where(columns < counts_ref[n, slot], tile, 0.0).astype(bf16)
            panel_ref[pl.ds(start, rows), n * tile_size : (n + 1) * tile_size] = kept
        return carry

    lax.fori_loop(0, slot_count, place, 0, unroll=8)


def dense_panel(places, counts, tiles, blocks_total):
    row_tiles, _, rows, tile_size = tiles.shape
    return pl.pallas_call(
        panel_kernel,
        out_shape=jax.ShapeDtypeStruct((blocks_total * rows, row_tiles * tile_size), bf16),
        in_specs=[
            pl.BlockSpec(memory_space=pltpu.SMEM),
            pl.BlockSpec(memory_space=pltpu.SMEM),
            pl.BlockSpec(memory_space=pltpu.VMEM),
        ],
        out_specs=pl.BlockSpec(memory_space=pltpu.VMEM),
        compiler_params=pltpu.CompilerParams(vmem_limit_bytes=16 * 1024 * 1024),
        cost_estimate=pl.CostEstimate(flops=0, bytes_accessed=4 * 1024 * 1024, transcendentals=0),
    )(places, counts, tiles)


def body(features, weight, cotangent, tile_values, tile_counts, tile_blocks):
    rows_dev, width = features.shape
    yh_n, z_n, x_n = (lax.axis_size(a) for a in BLK)
    rep_n = lax.axis_size(REP)
    shards = yh_n * z_n * x_n
    rep_index = lax.axis_index(REP)
    yh_index = lax.axis_index("yh")
    x_index = lax.axis_index("x")
    blocks = tile_blocks[0, 0]
    block_yh = blocks // (z_n * x_n)
    block_z = (blocks // x_n) % z_n
    places = (blocks % x_n) * (z_n * yh_n) + block_z * yh_n + block_yh
    panel = dense_panel(places, tile_counts[0, 0], tile_values[0, 0], shards)

    with jax.named_scope("gather_zy"):
        near = gather(features, ("z", "yh")).reshape(-1, width)
    section = near.shape[0]
    half = section // 2

    def product(distance, values, offset=0):
        start = ((x_index + distance) % x_n) * section + offset
        rows = lax.dynamic_slice_in_dim(panel, start, values.shape[0], 0)
        return lax.dot_general(
            rows, values, (((0,), (0,)), ((), ())), preferred_element_type=f32
        )

    with jax.named_scope("gather_x"):
        ahead = from_ahead(near, "x")
        behind = from_behind(near, "x")
        far_top = from_ahead(ahead[:half], "x")
        far_bottom = from_behind(behind[half:], "x")
    partial = product(0, near) + product(1, ahead) + product(3, behind)
    partial = partial + product(2, far_top) + product(2, far_bottom, half)
    yl_n, c_n = (lax.axis_size(a) for a in REP)
    yl_index, c_index = lax.axis_index("yl"), lax.axis_index("c")
    swap = [(0, 1), (1, 0)]
    with jax.named_scope("core_sum"):
        halves = partial.reshape(yl_n, c_n, rows_dev, width)
        kept = lax.dynamic_index_in_dim(halves, c_index, 1, keepdims=False)
        away = lax.dynamic_index_in_dim(halves, 1 - c_index, 1, keepdims=False)
        core_part = kept + lax.ppermute(away, "c", swap)
    with jax.named_scope("panel_sum"):
        parts = gather(core_part.astype(bf16), "yl")
        aggregate = jnp.sum(parts.astype(f32), axis=0).astype(bf16).reshape(-1, width)
    preact = jnp.dot(aggregate, weight, preferred_element_type=f32)
    sigmoid_value = jax.nn.sigmoid(preact)
    act_half = (preact * sigmoid_value).reshape(yl_n, rows_dev, width)
    activations = lax.dynamic_index_in_dim(act_half, yl_index, 0, keepdims=False).astype(bf16)
    own = lax.dynamic_index_in_dim(
        cotangent.reshape(yl_n, c_n, rows_dev, width), c_index, 1, keepdims=False
    )
    own = own.reshape(-1, width).astype(f32)
    slope = (own * sigmoid_value * (1.0 + preact * (1.0 - sigmoid_value))).astype(bf16)
    with jax.named_scope("core_swap"):
        other_slope = lax.ppermute(slope, "c", swap)
        other_aggregate = lax.ppermute(aggregate, "c", swap)
    first = jnp.where(c_index == 0, slope, other_slope).reshape(yl_n, rows_dev, width)
    second = jnp.where(c_index == 0, other_slope, slope).reshape(yl_n, rows_dev, width)
    panel_slope = jnp.stack([first, second], axis=1).reshape(-1, width)
    panel_back = lax.dot_general(
        panel_slope, weight, (((1,), (1,)), ((), ())), preferred_element_type=f32
    ).astype(bf16)
    weight_part = lax.dot_general(
        jnp.concatenate([aggregate, other_aggregate]),
        jnp.concatenate([slope, other_slope]),
        (((0,), (0,)), ((), ())),
        preferred_element_type=f32,
    )
    share = width // rep_n
    weight_rows = lax.dynamic_slice_in_dim(weight_part, rep_index * share, share, 0)
    contrib = jnp.dot(panel, panel_back, preferred_element_type=f32).astype(bf16)

    with jax.named_scope("sum_x"):
        parts = exchange(contrib.reshape(x_n, -1, width), "x")
        weight_rows = mirror_sum(pairwise_sum(weight_rows, "z", z_n // 2), "z")
        parts, weight_rows = lax.optimization_barrier((parts, weight_rows))
        from_x = jnp.sum(parts.astype(f32), axis=0).astype(bf16)
    with jax.named_scope("sum_z"):
        parts = exchange(from_x.reshape(z_n, -1, width), "z")
        weight_rows = pairwise_sum(pairwise_sum(weight_rows, "x", x_n), "yh", yh_n)
        copies = jnp.broadcast_to(weight_rows.astype(bf16), (rep_n, share, width))
        parts, copies = lax.optimization_barrier((parts, copies))
        halves = jnp.sum(parts.astype(f32), axis=0).reshape(yh_n, rows_dev, width)
    with jax.named_scope("weight_rep"):
        weight_all = exchange(copies, REP).reshape(width, width).astype(f32)
    with jax.named_scope("sum_y"):
        away = lax.dynamic_index_in_dim(halves, 1 - yh_index, 0, keepdims=False).astype(bf16)
        here = lax.dynamic_index_in_dim(halves, yh_index, 0, keepdims=False)
        arrived = lax.ppermute(away, "yh", [(0, 1), (1, 0)])
        grad_features = (here + arrived.astype(f32)).astype(bf16)
    node_total = rows_dev * shards * rep_n
    grad_weight = weight_all * float(node_total) ** (-0.5)
    return activations, grad_features, grad_weight


def solution(mesh):
    split = Mesh(mesh.devices.reshape(tuple(SPLIT.values())), tuple(SPLIT))
    return jax.shard_map(
        body,
        mesh=split,
        in_specs=(
            P(BLK + REP, None),
            P(),
            P(BLK, None),
            P(BLK, REP, None, None, None, None),
            P(BLK, REP, None, None),
            P(BLK, REP, None, None),
        ),
        out_specs=(P(BLK + REP, None), P(BLK + REP, None), P()),
        check_vma=False,
    )
```

```python
import jax
import jax.numpy as jnp
from jax import lax
from jax.experimental import pallas as pl
from jax.experimental.pallas import tpu as pltpu
from jax.sharding import Mesh, PartitionSpec as P

SPLIT = {"yh": 2, "z": 16, "x": 4, "yl": 4, "c": 2}
BLK = ("yh", "z", "x")
REP = ("yl", "c")
bf16 = jnp.bfloat16
f32 = jnp.float32


def exchange(chunks, axes):
    return lax.all_to_all(chunks, axes, 0, 0, tiled=True)


def gather(block, axes):
    members = lax.axis_size(axes)
    return exchange(jnp.broadcast_to(block, (members,) + block.shape), axes)


def from_ahead(value, axis):
    members = lax.axis_size(axis)
    return lax.ppermute(value, axis, [(i, (i - 1) % members) for i in range(members)])


def from_behind(value, axis):
    members = lax.axis_size(axis)
    return lax.ppermute(value, axis, [(i, (i + 1) % members) for i in range(members)])


def pairwise_sum(value, axis, members):
    stride = 1
    while stride < members:
        pairs = [(i, i ^ stride) for i in range(lax.axis_size(axis))]
        value = value + lax.ppermute(value, axis, pairs)
        stride *= 2
    return value


def mirror_sum(value, axis):
    members = lax.axis_size(axis)
    return value + lax.ppermute(value, axis, [(i, members - 1 - i) for i in range(members)])


def panel_kernel(places_ref, counts_ref, tiles_ref, panel_ref):
    row_tiles, slot_count, rows, tile_size = tiles_ref.shape
    total = panel_ref.shape[0]
    step = min(total, 256)

    def clear(i, carry):
        start = pl.multiple_of(i * step, step)
        panel_ref[pl.ds(start, step), :] = jnp.zeros((step, panel_ref.shape[1]), bf16)
        return carry

    lax.fori_loop(0, total // step, clear, 0)
    columns = lax.broadcasted_iota(jnp.int32, (rows, tile_size), 0)

    def place(slot, carry):
        for n in range(row_tiles):
            start = pl.multiple_of(places_ref[n, slot] * rows, rows)
            tile = tiles_ref[n, slot].astype(f32)
            kept = jnp.where(columns < counts_ref[n, slot], tile, 0.0).astype(bf16)
            panel_ref[pl.ds(start, rows), n * tile_size : (n + 1) * tile_size] = kept
        return carry

    lax.fori_loop(0, slot_count, place, 0, unroll=8)


def dense_panel(places, counts, tiles, blocks_total):
    row_tiles, _, rows, tile_size = tiles.shape
    return pl.pallas_call(
        panel_kernel,
        out_shape=jax.ShapeDtypeStruct((blocks_total * rows, row_tiles * tile_size), bf16),
        in_specs=[
            pl.BlockSpec(memory_space=pltpu.SMEM),
            pl.BlockSpec(memory_space=pltpu.SMEM),
            pl.BlockSpec(memory_space=pltpu.VMEM),
        ],
        out_specs=pl.BlockSpec(memory_space=pltpu.VMEM),
        compiler_params=pltpu.CompilerParams(vmem_limit_bytes=16 * 1024 * 1024),
        cost_estimate=pl.CostEstimate(flops=0, bytes_accessed=4 * 1024 * 1024, transcendentals=0),
    )(places, counts, tiles)


def body(features, weight, cotangent, tile_values, tile_counts, tile_blocks):
    rows_dev, width = features.shape
    yh_n, z_n, x_n = (lax.axis_size(a) for a in BLK)
    rep_n = lax.axis_size(REP)
    shards = yh_n * z_n * x_n
    rep_index = lax.axis_index(REP)
    yh_index = lax.axis_index("yh")
    x_index = lax.axis_index("x")
    blocks = tile_blocks[0, 0]
    block_yh = blocks // (z_n * x_n)
    block_z = (blocks // x_n) % z_n
    places = (blocks % x_n) * (z_n * yh_n) + block_z * yh_n + block_yh
    panel = dense_panel(places, tile_counts[0, 0], tile_values[0, 0], shards)

    with jax.named_scope("gather_zy"):
        near = gather(features, ("z", "yh")).reshape(-1, width)
    section = near.shape[0]
    half = section // 2

    def product(distance, values, offset=0):
        start = ((x_index + distance) % x_n) * section + offset
        rows = lax.dynamic_slice_in_dim(panel, start, values.shape[0], 0)
        return lax.dot_general(
            rows, values, (((0,), (0,)), ((), ())), preferred_element_type=f32
        )

    with jax.named_scope("gather_x"):
        near_top, near_bottom = near[:half], near[half:]
        ahead_top = from_ahead(near_top, "x")
        behind_bottom = from_behind(near_bottom, "x")
        ahead_bottom = from_ahead(near_bottom, "x")
        behind_top = from_behind(near_top, "x")
        far_top = from_ahead(ahead_top, "x")
        far_bottom = from_behind(behind_bottom, "x")
    partial = product(0, near) + product(1, ahead_top) + product(3, behind_bottom, half)
    partial = partial + product(1, ahead_bottom, half) + product(3, behind_top)
    partial = partial + product(2, far_top) + product(2, far_bottom, half)
    yl_n, c_n = (lax.axis_size(a) for a in REP)
    yl_index, c_index = lax.axis_index("yl"), lax.axis_index("c")
    swap = [(0, 1), (1, 0)]
    with jax.named_scope("core_sum"):
        halves = partial.reshape(yl_n, c_n, rows_dev, width)
        kept = lax.dynamic_index_in_dim(halves, c_index, 1, keepdims=False)
        away = lax.dynamic_index_in_dim(halves, 1 - c_index, 1, keepdims=False)
        core_part = kept + lax.ppermute(away, "c", swap)
    with jax.named_scope("panel_sum"):
        parts = gather(core_part.astype(bf16), "yl")
        aggregate = jnp.sum(parts.astype(f32), axis=0).astype(bf16).reshape(-1, width)
    preact = jnp.dot(aggregate, weight, preferred_element_type=f32)
    sigmoid_value = jax.nn.sigmoid(preact)
    act_half = (preact * sigmoid_value).reshape(yl_n, rows_dev, width)
    activations = lax.dynamic_index_in_dim(act_half, yl_index, 0, keepdims=False).astype(bf16)
    own = lax.dynamic_index_in_dim(
        cotangent.reshape(yl_n, c_n, rows_dev, width), c_index, 1, keepdims=False
    )
    own = own.reshape(-1, width).astype(f32)
    slope = (own * sigmoid_value * (1.0 + preact * (1.0 - sigmoid_value))).astype(bf16)
    with jax.named_scope("core_swap"):
        other_slope, other_aggregate = lax.ppermute(jnp.stack([slope, aggregate]), "c", swap)
    first = jnp.where(c_index == 0, slope, other_slope).reshape(yl_n, rows_dev, width)
    second = jnp.where(c_index == 0, other_slope, slope).reshape(yl_n, rows_dev, width)
    panel_slope = jnp.stack([first, second], axis=1).reshape(-1, width)
    panel_back = lax.dot_general(
        panel_slope, weight, (((1,), (1,)), ((), ())), preferred_element_type=f32
    ).astype(bf16)
    weight_part = lax.dot_general(
        jnp.concatenate([aggregate, other_aggregate]),
        jnp.concatenate([slope, other_slope]),
        (((0,), (0,)), ((), ())),
        preferred_element_type=f32,
    )
    share = width // rep_n
    weight_rows = lax.dynamic_slice_in_dim(weight_part, rep_index * share, share, 0)
    contrib = jnp.dot(panel, panel_back, preferred_element_type=f32).astype(bf16)

    with jax.named_scope("sum_x"):
        parts = exchange(contrib.reshape(x_n, -1, width), "x")
        weight_rows = mirror_sum(pairwise_sum(weight_rows, "z", z_n // 2), "z")
        parts, weight_rows = lax.optimization_barrier((parts, weight_rows))
        from_x = jnp.sum(parts.astype(f32), axis=0).astype(bf16)
    with jax.named_scope("sum_z"):
        parts = exchange(from_x.reshape(z_n, -1, width), "z")
        weight_rows = pairwise_sum(pairwise_sum(weight_rows, "x", x_n), "yh", yh_n)
        copies = jnp.broadcast_to(weight_rows.astype(bf16), (rep_n, share, width))
        parts, copies = lax.optimization_barrier((parts, copies))
        halves = jnp.sum(parts.astype(f32), axis=0).reshape(yh_n, rows_dev, width)
    with jax.named_scope("weight_rep"):
        weight_all = exchange(copies, REP).reshape(width, width).astype(f32)
    with jax.named_scope("sum_y"):
        away = lax.dynamic_index_in_dim(halves, 1 - yh_index, 0, keepdims=False).astype(bf16)
        here = lax.dynamic_index_in_dim(halves, yh_index, 0, keepdims=False)
        arrived = lax.ppermute(away, "yh", [(0, 1), (1, 0)])
        grad_features = (here + arrived.astype(f32)).astype(bf16)
    node_total = rows_dev * shards * rep_n
    grad_weight = weight_all * float(node_total) ** (-0.5)
    return activations, grad_features, grad_weight


def solution(mesh):
    split = Mesh(mesh.devices.reshape(tuple(SPLIT.values())), tuple(SPLIT))
    return jax.shard_map(
        body,
        mesh=split,
        in_specs=(
            P(BLK + REP, None),
            P(),
            P(BLK, None),
            P(BLK, REP, None, None, None, None),
            P(BLK, REP, None, None),
            P(BLK, REP, None, None),
        ),
        out_specs=(P(BLK + REP, None), P(BLK + REP, None), P()),
        check_vma=False,
    )
```

```python
import jax
import jax.numpy as jnp
from jax import lax
from jax.experimental import pallas as pl
from jax.experimental.pallas import tpu as pltpu
from jax.sharding import Mesh, PartitionSpec as P

SPLIT = {"yh": 2, "z": 16, "x": 4, "yl": 4, "c": 2}
BLK = ("yh", "z", "x")
REP = ("yl", "c")
bf16 = jnp.bfloat16
f32 = jnp.float32


def exchange(chunks, axes):
    return lax.all_to_all(chunks, axes, 0, 0, tiled=True)


def gather(block, axes):
    members = lax.axis_size(axes)
    return exchange(jnp.broadcast_to(block, (members,) + block.shape), axes)


def from_ahead(value, axis):
    members = lax.axis_size(axis)
    return lax.ppermute(value, axis, [(i, (i - 1) % members) for i in range(members)])


def from_behind(value, axis):
    members = lax.axis_size(axis)
    return lax.ppermute(value, axis, [(i, (i + 1) % members) for i in range(members)])


def pairwise_sum(value, axis, members):
    stride = 1
    while stride < members:
        pairs = [(i, i ^ stride) for i in range(lax.axis_size(axis))]
        value = value + lax.ppermute(value, axis, pairs)
        stride *= 2
    return value


def mirror_sum(value, axis):
    members = lax.axis_size(axis)
    return value + lax.ppermute(value, axis, [(i, members - 1 - i) for i in range(members)])


def panel_kernel(places_ref, counts_ref, tiles_ref, panel_ref):
    row_tiles, slot_count, rows, tile_size = tiles_ref.shape
    total = panel_ref.shape[0]
    step = min(total, 256)

    def clear(i, carry):
        start = pl.multiple_of(i * step, step)
        panel_ref[pl.ds(start, step), :] = jnp.zeros((step, panel_ref.shape[1]), bf16)
        return carry

    lax.fori_loop(0, total // step, clear, 0)
    columns = lax.broadcasted_iota(jnp.int32, (rows, tile_size), 0)

    def place(slot, carry):
        for n in range(row_tiles):
            start = pl.multiple_of(places_ref[n, slot] * rows, rows)
            tile = tiles_ref[n, slot].astype(f32)
            kept = jnp.where(columns < counts_ref[n, slot], tile, 0.0).astype(bf16)
            panel_ref[pl.ds(start, rows), n * tile_size : (n + 1) * tile_size] = kept
        return carry

    lax.fori_loop(0, slot_count, place, 0, unroll=8)


def dense_panel(places, counts, tiles, blocks_total):
    row_tiles, _, rows, tile_size = tiles.shape
    return pl.pallas_call(
        panel_kernel,
        out_shape=jax.ShapeDtypeStruct((blocks_total * rows, row_tiles * tile_size), bf16),
        in_specs=[
            pl.BlockSpec(memory_space=pltpu.SMEM),
            pl.BlockSpec(memory_space=pltpu.SMEM),
            pl.BlockSpec(memory_space=pltpu.VMEM),
        ],
        out_specs=pl.BlockSpec(memory_space=pltpu.VMEM),
        compiler_params=pltpu.CompilerParams(vmem_limit_bytes=16 * 1024 * 1024),
        cost_estimate=pl.CostEstimate(flops=0, bytes_accessed=4 * 1024 * 1024, transcendentals=0),
    )(places, counts, tiles)


def body(features, weight, cotangent, tile_values, tile_counts, tile_blocks):
    rows_dev, width = features.shape
    yh_n, z_n, x_n = (lax.axis_size(a) for a in BLK)
    rep_n = lax.axis_size(REP)
    shards = yh_n * z_n * x_n
    rep_index = lax.axis_index(REP)
    yh_index = lax.axis_index("yh")
    x_index = lax.axis_index("x")
    blocks = tile_blocks[0, 0]
    block_yh = blocks // (z_n * x_n)
    block_z = (blocks // x_n) % z_n
    places = (blocks % x_n) * (z_n * yh_n) + block_z * yh_n + block_yh
    panel = dense_panel(places, tile_counts[0, 0], tile_values[0, 0], shards)

    with jax.named_scope("gather_zy"):
        near = gather(features, ("z", "yh")).reshape(-1, width)
    section = near.shape[0]
    half = section // 2

    def product(distance, values, offset=0):
        start = ((x_index + distance) % x_n) * section + offset
        rows = lax.dynamic_slice_in_dim(panel, start, values.shape[0], 0)
        return lax.dot_general(
            rows, values, (((0,), (0,)), ((), ())), preferred_element_type=f32
        )

    with jax.named_scope("gather_x"):
        near_top, near_bottom = near[:half], near[half:]
        ahead_top = from_ahead(near_top, "x")
        behind_bottom = from_behind(near_bottom, "x")
        ahead_bottom = from_ahead(near_bottom, "x")
        behind_top = from_behind(near_top, "x")
        far_top = from_ahead(ahead_top, "x")
        far_bottom = from_behind(behind_bottom, "x")
    partial = product(0, near) + product(1, ahead_top) + product(3, behind_bottom, half)
    partial = partial + product(1, ahead_bottom, half) + product(3, behind_top)
    partial = partial + product(2, far_top) + product(2, far_bottom, half)
    yl_n, c_n = (lax.axis_size(a) for a in REP)
    yl_index, c_index = lax.axis_index("yl"), lax.axis_index("c")
    swap = [(0, 1), (1, 0)]
    with jax.named_scope("core_sum"):
        halves = partial.reshape(yl_n, c_n, rows_dev, width)
        kept = lax.dynamic_index_in_dim(halves, c_index, 1, keepdims=False)
        away = lax.dynamic_index_in_dim(halves, 1 - c_index, 1, keepdims=False)
        core_part = kept + lax.ppermute(away, "c", swap)
    with jax.named_scope("panel_sum"):
        parts = gather(core_part.astype(bf16), "yl")
        aggregate = jnp.sum(parts.astype(f32), axis=0).astype(bf16).reshape(-1, width)
    preact = jnp.dot(aggregate, weight, preferred_element_type=f32)
    sigmoid_value = jax.nn.sigmoid(preact)
    act_half = (preact * sigmoid_value).reshape(yl_n, rows_dev, width)
    activations = lax.dynamic_index_in_dim(act_half, yl_index, 0, keepdims=False).astype(bf16)
    own = lax.dynamic_index_in_dim(
        cotangent.reshape(yl_n, c_n, rows_dev, width), c_index, 1, keepdims=False
    )
    own = own.reshape(-1, width).astype(f32)
    slope = (own * sigmoid_value * (1.0 + preact * (1.0 - sigmoid_value))).astype(bf16)
    with jax.named_scope("core_swap"):
        other_slope, other_aggregate = lax.ppermute(jnp.stack([slope, aggregate]), "c", swap)
    first = jnp.where(c_index == 0, slope, other_slope).reshape(yl_n, rows_dev, width)
    second = jnp.where(c_index == 0, other_slope, slope).reshape(yl_n, rows_dev, width)
    panel_slope = jnp.stack([first, second], axis=1).reshape(-1, width)
    panel_back = lax.dot_general(
        panel_slope, weight, (((1,), (1,)), ((), ())), preferred_element_type=f32
    ).astype(bf16)
    weight_part = lax.dot_general(
        jnp.concatenate([aggregate, other_aggregate]),
        jnp.concatenate([slope, other_slope]),
        (((0,), (0,)), ((), ())),
        preferred_element_type=f32,
    )
    share = width // rep_n
    weight_rows = lax.dynamic_slice_in_dim(weight_part, rep_index * share, share, 0)
    contrib = jnp.dot(panel, panel_back, preferred_element_type=f32).astype(bf16)

    with jax.named_scope("sum_x"):
        parts = exchange(contrib.reshape(x_n, -1, width), "x")
        weight_rows = pairwise_sum(weight_rows, "z", z_n // 2)
        parts, weight_rows = lax.optimization_barrier((parts, weight_rows))
        from_x = jnp.sum(parts.astype(f32), axis=0).astype(bf16)
    with jax.named_scope("sum_z"):
        parts = exchange(from_x.reshape(z_n, -1, width), "z")
        weight_rows = pairwise_sum(pairwise_sum(weight_rows, "x", x_n), "yh", yh_n)
        weight_rows = mirror_sum(weight_rows, "z")
        copies = jnp.broadcast_to(weight_rows.astype(bf16), (rep_n, share, width))
        halves = jnp.sum(parts.astype(f32), axis=0).reshape(yh_n, rows_dev, width)
    with jax.named_scope("weight_rep"):
        weight_all = exchange(copies, REP).reshape(width, width).astype(f32)
    with jax.named_scope("sum_y"):
        away = lax.dynamic_index_in_dim(halves, 1 - yh_index, 0, keepdims=False).astype(bf16)
        here = lax.dynamic_index_in_dim(halves, yh_index, 0, keepdims=False)
        arrived = lax.ppermute(away, "yh", [(0, 1), (1, 0)])
        grad_features = (here + arrived.astype(f32)).astype(bf16)
    node_total = rows_dev * shards * rep_n
    grad_weight = weight_all * float(node_total) ** (-0.5)
    return activations, grad_features, grad_weight


def solution(mesh):
    split = Mesh(mesh.devices.reshape(tuple(SPLIT.values())), tuple(SPLIT))
    return jax.shard_map(
        body,
        mesh=split,
        in_specs=(
            P(BLK + REP, None),
            P(),
            P(BLK, None),
            P(BLK, REP, None, None, None, None),
            P(BLK, REP, None, None),
            P(BLK, REP, None, None),
        ),
        out_specs=(P(BLK + REP, None), P(BLK + REP, None), P()),
        check_vma=False,
    )
```
